32 devices in a mesh: row: 4 (over y, x), col: 4 (over z), freq: 2 (over core).
Axes of the slice: x: 2, y: 2, z: 4, core: 2. Of those that a mesh axis runs over, the one named last changes fastest.
Arguments:
- visibility: bfloat16 [16, 8, 16, 64, 128], P(('row', 'col'), None, 'freq'), may hold values from -6 to 6
- tasks: int32 [16, 3], P(('row', 'col')), may hold values from 0 to 3, as said below
- flags: int32 [16, 256], P(None, ('row', 'col')), may hold values 0 or 1
- station_uvw: float32 [16, 3, 256], replicated, may hold values from -256 to 256
- comp_lm: float32 [2, 512], replicated, may hold values from -0.08 to 0.08
- intensity: float32 [512], replicated, may hold values from 0.02 to 0.2
- direction: int32 [512], replicated, may hold values from 0 to 7, as said below
- coefs: float32 [4, 2, 8, 256], P(None, None, None, ('row', 'col')), may hold values from -6 to 6
Outputs:
- gradient: float32 [4, 2, 8, 256], P(None, None, None, ('row', 'col'))
The draws below stay inside these ranges and needn't reach their ends.
Inputs may be any that keep to these rules, and one draw needn't show every extreme that they name: Each row of tasks is (bi, bj, h) with bi <= bj: h is 0 or 1 when bi < bj and 2 when bi == bj; every pair bi < bj appears with h = 0 and with h = 1, and every block with h = 2, each exactly once, in an order drawn from the seed. Every direction holds exactly 64 components.
All inputs are finite; a program needn't handle non-finite values. No bound on the sum of `flags` on one device may be relied on, other than what follows from the above.
Results may differ from the reference program's by a relative error of at most 0.0003.
Values sent between devices are 32-bit elements; how exact they have to be, the bound alone decides.
A program may use at most 64 MiB of HBM per device.

```python
import math
import jax
import jax.numpy as jnp
from jax import lax

SB = 64
NB = 4
S = 256
TASKS = 16
D = 8
COMP = 64
K = 512
CH = 16
NP = 4
TH = 8
INTS = 16


def draw_tasks(key, part):
    key = jax.random.fold_in(key, 11)
    first = jnp.arange(NB, dtype=jnp.int32)[:, None] * jnp.ones((1, NB), jnp.int32)
    second = jnp.transpose(first)
    smaller = jnp.minimum(first, second)
    larger = jnp.maximum(first, second)
    kinds = jnp.where(first < second, 0, jnp.where(first > second, 1, 2)).astype(jnp.int32)
    table = jnp.stack([smaller, larger, kinds], axis=-1).reshape(NB * NB, 3)
    order = jax.random.permutation(key, NB * NB)
    return table[order].astype(jnp.int32)


def draw_direction(key, part):
    key = jax.random.fold_in(key, 23)
    order = jax.random.permutation(key, K).astype(jnp.int32)
    return (order // COMP).astype(jnp.int32)


def touch_ends(entries, own_key, least, high):
    longest = entries.shape.index(max(entries.shape))
    spots = []
    for shift in (0, 1):
        where = [jax.random.randint(jax.random.fold_in(own_key, axis), (), 0, length) for axis, length in enumerate(entries.shape)]
        where[longest] = (where[longest] + shift) % entries.shape[longest]
        spots.append(tuple(where))
    return entries.at[spots[0]].set(least).at[spots[1]].set(high)


def block_scale(rng, shape, split, low, largest):
    def one(dim, shards_of):
        steps = jax.random.uniform(jax.random.fold_in(jax.random.fold_in(rng, 6), dim), (shards_of,), jnp.float32, low / len(split), largest / len(split))
        return jnp.repeat(jnp.exp(steps), shape[dim] // shards_of).reshape((-1,) + (1,) * (len(shape) - dim - 1))

    factor_of = one(*split[0])
    for cut in split[1:]:
        factor_of = factor_of * one(*cut)
    return factor_of


def noise(key, extent, deviation, reach, split=(), kind=jnp.bfloat16):
    drawn = deviation * jax.random.normal(key, extent, jnp.float32)
    if split:
        drawn = drawn * block_scale(key, extent, split, -0.22, 0.18)
    return jnp.clip(drawn, -reach, reach).astype(kind)


def setup_inputs(seed: int = 0) -> dict:
    streams_of = jax.random.split(jax.random.key(seed), 9)
    visibility = noise(streams_of[0], (TASKS, TH, CH, SB, 2 * SB), 1.0, 6.0, ((0, 16), (2, 2)))
    tasks = draw_tasks(jax.random.fold_in(streams_of[8], 71), 0)
    flags = touch_ends((jax.random.randint(streams_of[2], (INTS, S), 0, 8) < 7).astype(jnp.int32), jax.random.fold_in(streams_of[2], 1), 0, 1)
    station_uvw = noise(streams_of[3], (INTS, 3, S), 40.0, 256.0, (), jnp.float32)
    comp_lm = jnp.clip(jax.random.uniform(streams_of[4], (2, K), jnp.float32, -0.08, 0.08), -0.08, 0.08)
    intensity = jnp.clip(jnp.exp(jax.random.uniform(streams_of[5], (K,), jnp.float32, math.log(0.02), math.log(0.2))), 0.02, 0.2)
    direction = draw_direction(jax.random.fold_in(streams_of[8], 71), 0)
    coefs = noise(streams_of[7], (NP, 2, D, S), 0.5, 6.0, ((3, 16),), jnp.float32)
    return {"visibility": visibility, "tasks": tasks, "flags": flags, "station_uvw": station_uvw, "comp_lm": comp_lm, "intensity": intensity, "direction": direction, "coefs": coefs}


highest = lax.Precision.HIGHEST

def channel_grid(count):
    return (2.0 * jnp.arange(count, dtype=jnp.float32) - (count - 1)) / (count - 1)

def poly_gains(coefs, points):
    total = jnp.zeros((points.shape[0],) + coefs.shape[1:], jnp.float32)
    for order in range(coefs.shape[0]):
        total = total + (points ** order)[:, None, None, None] * coefs[order][None]
    return total

def project_poly(values, points, orders):
    return jnp.stack([jnp.einsum('f,frdn->rdn', points ** order, values, precision=highest) for order in range(orders)])

def make_onehot(direction, count):
    return (direction[:, None] == jnp.arange(count, dtype=jnp.int32)[None, :]).astype(jnp.float32)

def phase_tables(uvw_cols, comp_lm, factor):
    sky_east = comp_lm[0]
    sky_north = comp_lm[1]
    sky_depth = jnp.sqrt(1.0 - sky_east * sky_east - sky_north * sky_north) - 1.0
    projected = uvw_cols[0][:, None] * sky_east[None, :] + uvw_cols[1][:, None] * sky_north[None, :] + uvw_cols[2][:, None] * sky_depth[None, :]
    angle = 2.0 * math.pi * factor * projected
    return (jnp.cos(angle), jnp.sin(angle))

def dot_rows(left, right):
    return lax.dot_general(left, right, (((1,), (1,)), ((), ())), preferred_element_type=jnp.float32)

def dot_cols(left, right):
    return lax.dot_general(left, right, (((0,), (0,)), ((), ())), preferred_element_type=jnp.float32)

def block_pass(vis_pair, weight, row_uvw, col_uvw, row_gain, col_gain, comp_lm, intensity, onehot, point):
    factor = 1.0 + 0.15 * point
    row_cos, row_sin = phase_tables(row_uvw, comp_lm, factor)
    col_cos, col_sin = phase_tables(col_uvw, comp_lm, factor)
    left_real = ((row_gain[0] * row_cos + row_gain[1] * row_sin) * intensity).astype(jnp.bfloat16)
    left_imag = ((row_gain[1] * row_cos - row_gain[0] * row_sin) * intensity).astype(jnp.bfloat16)
    right_real = (col_gain[0] * col_cos + col_gain[1] * col_sin).astype(jnp.bfloat16)
    right_imag = (col_gain[1] * col_cos - col_gain[0] * col_sin).astype(jnp.bfloat16)
    left_both = jnp.concatenate([left_real, left_imag], axis=1)
    model_real = dot_rows(left_both, jnp.concatenate([right_real, right_imag], axis=1))
    model_imag = dot_rows(left_both, jnp.concatenate([-right_imag, right_real], axis=1))
    width = vis_pair.shape[1] // 2
    resid_real = (weight * (vis_pair[:, :width].astype(jnp.float32) - model_real)).astype(jnp.bfloat16)
    resid_imag = (weight * (vis_pair[:, width:].astype(jnp.float32) - model_imag)).astype(jnp.bfloat16)
    toward_real = jnp.dot(resid_real, right_real, preferred_element_type=jnp.float32) - jnp.dot(resid_imag, right_imag, preferred_element_type=jnp.float32)
    toward_imag = jnp.dot(resid_real, right_imag, preferred_element_type=jnp.float32) + jnp.dot(resid_imag, right_real, preferred_element_type=jnp.float32)
    row_real = intensity * (row_cos * toward_real - row_sin * toward_imag)
    row_imag = intensity * (row_cos * toward_imag + row_sin * toward_real)
    back_real = dot_cols(resid_real, left_real) + dot_cols(resid_imag, left_imag)
    back_imag = dot_cols(resid_real, left_imag) - dot_cols(resid_imag, left_real)
    col_real = col_cos * back_real - col_sin * back_imag
    col_imag = col_cos * back_imag + col_sin * back_real
    row_terms = -jnp.stack([jnp.dot(row_real, onehot, precision=highest), jnp.dot(row_imag, onehot, precision=highest)])
    col_terms = -jnp.stack([jnp.dot(col_real, onehot, precision=highest), jnp.dot(col_imag, onehot, precision=highest)])
    return (row_terms, col_terms)

def task_terms(vis_task, entry, flag_all, station_uvw, comp_lm, intensity, onehot, gains, points):
    block = vis_task.shape[2]
    half = vis_task.shape[0]
    row_start = (entry[0] * block).astype(jnp.int32)
    col_start = (entry[1] * block).astype(jnp.int32)
    kind = entry[2]
    row_gains = jnp.einsum('crds,kd->crsk', lax.dynamic_slice_in_dim(gains, row_start, block, 3), onehot, precision=highest)
    col_gains = jnp.einsum('crds,kd->crsk', lax.dynamic_slice_in_dim(gains, col_start, block, 3), onehot, precision=highest)
    row_flags = lax.dynamic_slice_in_dim(flag_all, row_start, block, 1)
    col_flags = lax.dynamic_slice_in_dim(flag_all, col_start, block, 1)
    row_uvw = lax.dynamic_slice_in_dim(station_uvw, row_start, block, 2)
    col_uvw = lax.dynamic_slice_in_dim(station_uvw, col_start, block, 2)
    across = jnp.arange(block, dtype=jnp.int32)
    upper = (across[:, None] < across[None, :]).astype(jnp.float32)
    lower = (across[:, None] > across[None, :]).astype(jnp.float32)
    first_mask = jnp.where(kind == 2, upper, jnp.ones_like(upper))
    channel_pass = jax.vmap(block_pass, in_axes=(0, None, None, None, 0, 0, None, None, None, 0))

    def pass_at(vis_time, moment, mask):
        weight = row_flags[moment][:, None] * col_flags[moment][None, :] * mask
        return channel_pass(vis_time, weight, row_uvw[moment], col_uvw[moment], row_gains, col_gains, comp_lm, intensity, onehot, points)

    def one_time(carry, item):
        vis_time, moment = item
        first_row, first_col = pass_at(vis_time, moment + half * (kind == 1).astype(jnp.int32), first_mask)

        def with_second(unused):
            second_row, second_col = pass_at(vis_time, moment + half, lower)
            return (first_row + second_row, first_col + second_col)

        def alone(unused):
            return (first_row, first_col)
        row_terms, col_terms = lax.cond(kind == 2, with_second, alone, 0)
        return ((carry[0] + row_terms, carry[1] + col_terms), None)
    zeros = jnp.zeros((points.shape[0], 2, block, onehot.shape[1]), jnp.float32)
    sums, unused = lax.scan(one_time, (zeros, zeros), (vis_task, jnp.arange(half, dtype=jnp.int32)))
    return (jnp.swapaxes(sums[0], 2, 3), jnp.swapaxes(sums[1], 2, 3), row_start, col_start)

def add_block(total, piece, start):
    last = total.ndim - 1
    current = lax.dynamic_slice_in_dim(total, start, piece.shape[last], last)
    return lax.dynamic_update_slice_in_dim(total, current + piece, start, last)

def reference(visibility, tasks, flags, station_uvw, comp_lm, intensity, direction, coefs):
    points = channel_grid(CH)
    onehot = make_onehot(direction, D)
    gains = poly_gains(coefs, points)
    flag_all = flags.astype(jnp.float32)

    def one_task(total, item):
        vis_task, entry = item
        row_part, col_part, row_start, col_start = task_terms(vis_task, entry, flag_all, station_uvw, comp_lm, intensity, onehot, gains, points)
        total = add_block(add_block(total, row_part, row_start), col_part, col_start)
        return (total, None)
    total, unused = lax.scan(one_task, jnp.zeros((CH, 2, D, S), jnp.float32), (visibility, tasks))
    return project_poly(total, points, NP) * (1.0 / math.sqrt(2 * TH * CH * S))
```

```python
import functools
import math

import jax
import jax.numpy as jnp
import numpy as np
from jax import lax
from jax.experimental import pallas as pl
from jax.experimental.pallas import tpu as pltpu
from jax.sharding import PartitionSpec as P

MESH = pl.DeviceIdType.MESH
LANES = 128
F32 = jnp.float32


def fit_even(function, terms):
    nodes = 0.25 * (1.0 - np.cos(np.pi * (np.arange(400) + 0.5) / 400)) / 2.0
    values = function(np.sqrt(nodes))
    basis = np.stack([nodes**n for n in range(terms)], axis=1)
    return [float(c) for c in np.linalg.lstsq(basis, values, rcond=None)[0]]


SIN_FIT = fit_even(lambda r: np.sin(np.pi * r) / r, 5)
COS_FIT = fit_even(lambda r: np.cos(np.pi * r), 6)


def horner(coefficients, z):
    total = jnp.full_like(z, coefficients[-1])
    for c in coefficients[-2::-1]:
        total = total * z + c
    return total


def turn_cos_sin(turns):
    r = turns - jnp.round(turns)
    z = r * r
    s = horner(SIN_FIT, z) * r
    c = horner(COS_FIT, z)
    return 1.0 - 2.0 * (s * s), 2.0 * (s * c)


def others(sizes, axes, body):
    count = math.prod(sizes)
    me = 0
    for size, axis in zip(sizes, axes):
        me = me * size + lax.axis_index(axis)

    def step(j, unused):
        rest = lax.rem(me + j + 1, count)
        where = {}
        for size, axis in zip(sizes[::-1], axes[::-1]):
            where[axis] = lax.rem(rest, size)
            rest = rest // size
        body(j, where)
        return unused

    lax.fori_loop(0, count - 1, step, 0)
    return me


def greet(sizes, axes):
    barrier = pltpu.get_barrier_semaphore()

    def signal(j, where):
        pl.semaphore_signal(barrier, inc=1, device_id=where, device_id_type=MESH)

    me = others(sizes, axes, signal)
    pl.semaphore_wait(barrier, math.prod(sizes) - 1)
    return me


def put_lanes(piece, start):
    rows, width = piece.shape
    parts = []
    if start:
        parts.append(jnp.zeros((rows, start), piece.dtype))
    parts.append(piece)
    if start + width < LANES:
        parts.append(jnp.zeros((rows, LANES - start - width), piece.dtype))
    return jnp.concatenate(parts, axis=1) if len(parts) > 1 else piece


def gather_kernel(sizes, coef_ref, flag_ref, all_ref, mine, send_sem, recv_sem, own_sem):
    axes = ("row", "col")
    width = coef_ref.shape[1]
    for base, ref in ((0, coef_ref), (8, flag_ref)):
        tile = jnp.zeros((8, LANES), F32)
        for g in range(ref.shape[0] // 8):
            tile = tile + put_lanes(ref[8 * g : 8 * g + 8, :].astype(F32), g * width)
        mine[base : base + 8, :] = tile
    me = greet(sizes, axes)

    def send(j, where):
        pltpu.make_async_remote_copy(
            src_ref=mine,
            dst_ref=all_ref.at[me],
            send_sem=send_sem,
            recv_sem=recv_sem,
            device_id=where,
            device_id_type=MESH,
        ).start()

    others(sizes, axes, send)
    own = pltpu.make_async_copy(mine, all_ref.at[me], own_sem)
    own.start()
    own.wait()
    rest = all_ref.at[pl.ds(0, math.prod(sizes) - 1)]
    done = pltpu.make_async_remote_copy(
        src_ref=rest,
        dst_ref=rest,
        send_sem=send_sem,
        recv_sem=recv_sem,
        device_id={axis: lax.axis_index(axis) for axis in axes},
        device_id_type=MESH,
    )
    done.wait_send()
    done.wait_recv()


def reduce_kernel(sizes, part_ref, out_ref, held, send_sem, recv_sem):
    axes = ("row", "col", "freq")
    me = greet(sizes, axes)
    groups = sizes[2]

    def send(j, where):
        owner = where["row"] * sizes[1] + where["col"]
        pltpu.make_async_remote_copy(
            src_ref=part_ref.at[owner],
            dst_ref=held.at[j],
            send_sem=send_sem,
            recv_sem=recv_sem,
            device_id=where,
            device_id_type=MESH,
        ).start()

    others(sizes, axes, send)
    done = pltpu.make_async_remote_copy(
        src_ref=held,
        dst_ref=held,
        send_sem=send_sem,
        recv_sem=recv_sem,
        device_id={axis: lax.axis_index(axis) for axis in axes},
        device_id_type=MESH,
    )
    done.wait_send()
    done.wait_recv()
    total = part_ref[me // groups] + jnp.sum(held[...], axis=0)
    width = out_ref.shape[1]
    for g in range(out_ref.shape[0] // 8):
        out_ref[8 * g : 8 * g + 8, :] = total[:, g * width : (g + 1) * width]


def halves_swapped(x):
    return jnp.concatenate([x[:, LANES // 2 :], x[:, : LANES // 2]], axis=1)


def work_kernel(
    width,
    channels,
    task_ref,
    point_ref,
    all_ref,
    vis_ref,
    uvw_ref,
    lm_ref,
    intensity_ref,
    direction_ref,
    out_ref,
    gains,
    flags,
    sky,
    weight,
    step_table,
    phase,
    x_ref,
    sums,
):
    times, local, block = vis_ref.shape[0], vis_ref.shape[1], vis_ref.shape[2]
    comps = sky.shape[1]
    directions = gains.shape[2]
    each = comps // directions
    orders = 4
    owners = block // width
    first, second, kind = task_ref[0, 0], task_ref[0, 1], task_ref[0, 2]
    paired = kind == 2
    lane = lax.broadcasted_iota(jnp.int32, (8, LANES), 1)
    on_a = lane < block

    for g in range(2 * orders + flags.shape[0] // 8):
        base, at = (0, g) if g < 2 * orders else (8, g - 2 * orders)
        tile = jnp.zeros((8, LANES), F32)
        for side, blk in ((0, first), (1, second)):
            for i in range(owners):
                piece = all_ref[blk * owners + i, base : base + 8, at * width : (at + 1) * width]
                tile = tile + put_lanes(piece, side * block + i * width)
        if g < 2 * orders:
            sums[0, 0, g] = tile
        else:
            flags[8 * at : 8 * at + 8, :] = tile
    for f in range(local):
        x = point_ref[0, f]
        for c in range(2):
            value = sums[0, 0, 2 * orders - 2 + c]
            for n in range(orders - 2, -1, -1):
                value = value * x + sums[0, 0, 2 * n + c]
            gains[f, c] = value

    drow = direction_ref[...].astype(F32)
    count = jnp.zeros((1, comps), F32)
    krow = lax.broadcasted_iota(jnp.int32, (LANES, comps), 1)
    jcol = lax.broadcasted_iota(jnp.int32, (LANES, comps), 0)
    for j in range(comps // LANES):
        piece = jnp.broadcast_to(drow[:, j * LANES : (j + 1) * LANES], (LANES, LANES))
        column = jnp.transpose(piece)
        column = jnp.concatenate([column] * (comps // LANES), axis=1)
        same = jnp.logical_and(column == drow, jcol + j * LANES < krow)
        count = count + jnp.sum(same.astype(F32), axis=0, keepdims=True)
    place = (drow * each + count).astype(jnp.int32)
    east, north = lm_ref[0:1, :], lm_ref[1:2, :]
    depth = jnp.sqrt(1.0 - east * east - north * north) - 1.0
    bright = intensity_ref[...]
    for d in range(directions):
        rows = pl.ds(d * each, each)
        here = lax.broadcasted_iota(jnp.int32, (each, comps), 0) + d * each == place
        for n, value in enumerate((east, north, depth, bright)):
            column = jnp.sum(jnp.where(here, value, 0.0), axis=1, keepdims=True)
            if n < 3:
                sky[n, rows, :] = jnp.broadcast_to(column, (each, LANES))
            else:
                wide = jnp.broadcast_to(column, (each, LANES))
                mixed = lax.broadcasted_iota(jnp.int32, (each, LANES), 1) < block
                sky[3, rows, :] = jnp.where(paired, jnp.sqrt(wide), jnp.where(mixed, wide, 1.0))

    i = lax.broadcasted_iota(jnp.int32, (block, LANES), 0)
    j = lax.broadcasted_iota(jnp.int32, (block, LANES), 1)
    left = j < block
    j = jnp.where(left, j, j - block)
    one, zero = jnp.float32(1.0), jnp.float32(0.0)
    upper = (i < j).astype(F32)
    lower = (i > j).astype(F32)
    leftf = left.astype(F32)
    pick_a = jnp.where(paired, upper, one)
    pick_b = jnp.where(paired, lower, zero)
    unequal = upper + lower
    mask_a = jnp.where(paired, unequal * leftf, 1.0 - leftf)
    mask_b = jnp.where(paired, unequal * (1.0 - leftf), leftf)

    sums[...] = jnp.zeros_like(sums)
    late_a = jnp.where(kind == 1, times, 0)
    late_b = jnp.where(kind == 0, 0, times)
    factor = 1.0 + 0.15 * point_ref[0, 0]
    spacing = 0.15 * 2.0 / (channels - 1)

    def side_tile(ref, blk, side, moment):
        tile = ref[moment, :, pl.ds(pl.multiple_of((blk // 2) * LANES, LANES), LANES)]
        return jnp.where(lax.rem(blk, 2) == side, tile, halves_swapped(tile))

    def make_x(f, slot):
        for d in range(directions):
            rows = pl.ds(d * each, each)
            if f == 0:
                c, s = phase[0, 0, rows, :], phase[0, 1, rows, :]
            else:
                c0, s0 = phase[1 - slot, 0, rows, :], phase[1 - slot, 1, rows, :]
                ec, es = step_table[0, rows, :], step_table[1, rows, :]
                c = c0 * ec - s0 * es
                s = s0 * ec + c0 * es
                phase[slot, 0, rows, :] = c
                phase[slot, 1, rows, :] = s
            gr, gi = gains[f, 0, d : d + 1, :], gains[f, 1, d : d + 1, :]
            x_ref[slot, rows, 0:LANES] = (gr * c + gi * s).astype(jnp.bfloat16)
            x_ref[slot, rows, LANES : 2 * LANES] = (gi * c - gr * s).astype(jnp.bfloat16)

    def one_time(t, unused):
        tau_a, tau_b = t + late_a, t + late_b
        uvw = jnp.where(
            lax.broadcasted_iota(jnp.int32, (3, LANES), 1) < block,
            side_tile(uvw_ref, first, 0, tau_a),
            side_tile(uvw_ref, second, 1, tau_b),
        )
        good = jnp.where(
            lax.broadcasted_iota(jnp.int32, (1, LANES), 1) < block,
            flags[pl.ds(tau_a, 1), :],
            flags[pl.ds(tau_b, 1), :],
        )
        good = jnp.broadcast_to(good, (LANES, LANES))
        both = good * jnp.transpose(good)
        weight[0:block, :] = both[0:block] * mask_a
        weight[block : 2 * block, :] = both[block : 2 * block] * mask_b
        for d in range(directions):
            rows = pl.ds(d * each, each)
            turns = (
                sky[0, rows, :] * uvw[0:1] + sky[1, rows, :] * uvw[1:2] + sky[2, rows, :] * uvw[2:3]
            )
            c, s = turn_cos_sin(turns * factor)
            phase[0, 0, rows, :] = c * sky[3, rows, :]
            phase[0, 1, rows, :] = s * sky[3, rows, :]
            c, s = turn_cos_sin(turns * spacing)
            step_table[0, rows, :] = c
            step_table[1, rows, :] = s
        make_x(0, 0)
        for f in range(local):
            slot = f % 2
            x = x_ref[slot]
            z = lax.dot_general(x, x, (((0,), (0,)), ((), ())), preferred_element_type=F32)
            if f + 1 < local:
                make_x(f + 1, 1 - slot)
            v = vis_ref[t, f].astype(F32)
            turned = jnp.transpose(jnp.concatenate([v, v], axis=0))
            swapped = halves_swapped(v)
            real, imag = jnp.where(left, v, swapped), jnp.where(left, swapped, v)
            model_r = z[0:LANES, 0:LANES] + z[LANES:, LANES:]
            model_i = z[0:LANES, LANES:] - z[LANES:, 0:LANES]
            parts_r, parts_i = [], []
            for side, pick in ((0, pick_a), (1, pick_b)):
                rows = slice(side * block, (side + 1) * block)
                want = pick > 0.5
                vr = jnp.where(want, real, turned[0:block])
                vi = jnp.where(want, -imag, turned[block:])
                w = weight[rows, :]
                parts_r.append(w * (vr - model_r[rows]))
                parts_i.append(w * (vi - model_i[rows]))
            er = jnp.concatenate(parts_r, axis=0).astype(jnp.bfloat16)
            ei = jnp.concatenate(parts_i, axis=0).astype(jnp.bfloat16)
            e = jnp.concatenate(
                [jnp.concatenate([er, ei], axis=1), jnp.concatenate([-ei, er], axis=1)], axis=0
            )
            h = jnp.dot(x, e, preferred_element_type=F32)
            for d in range(directions):
                rows = slice(d * each, (d + 1) * each)
                c, s = phase[slot, 0, rows, :], phase[slot, 1, rows, :]
                hr, hi = h[rows, 0:LANES], h[rows, LANES:]
                tr = jnp.sum((c * hr - s * hi).reshape(each // 8, 8, LANES), axis=0)
                ti = jnp.sum((c * hi + s * hr).reshape(each // 8, 8, LANES), axis=0)
                sums[f, 0, d] += tr
                sums[f, 1, d] += ti
        return unused

    lax.fori_loop(0, times, one_time, 0)

    scale = -1.0 / math.sqrt(2 * times * channels * out_ref.shape[0] * width)
    out_ref[...] = jnp.zeros_like(out_ref)
    tiles = [None] * (2 * orders)
    for f in range(local):
        x = point_ref[0, f]
        for c in range(2):
            total = jnp.sum(sums[f, c], axis=1) * scale
            for n in range(orders):
                old = tiles[2 * n + c]
                tiles[2 * n + c] = total if old is None else old + total
                total = total * x
    for side, blk in ((0, first), (1, second)):
        for i in range(owners):
            start = side * block + i * width
            packed = [tiles[g][:, start : start + width] for g in range(2 * orders)]
            tile = jnp.concatenate(packed, axis=1)
            out_ref[blk * owners + i] += put_lanes(tile, 0)


def vmem():
    return pl.BlockSpec(memory_space=pltpu.VMEM)


def smem():
    return pl.BlockSpec(memory_space=pltpu.SMEM)


def on_device(sizes, visibility, tasks, flags, station_uvw, comp_lm, intensity, direction, coefs):
    rows, cols, parts = sizes
    devices = rows * cols
    orders, unused, directions, width = coefs.shape
    unused, times, local, block, unused = visibility.shape
    comps = direction.shape[0]
    channels = local * parts
    offset = lax.axis_index("freq") * local
    points = (
        2.0 * (offset + jnp.arange(local, dtype=jnp.int32)).astype(F32) - (channels - 1)
    ) / (channels - 1)

    gathered = pl.pallas_call(
        functools.partial(gather_kernel, (rows, cols)),
        out_shape=jax.ShapeDtypeStruct((devices, 16, LANES), F32),
        in_specs=[vmem()] * 2,
        out_specs=vmem(),
        scratch_shapes=[
            pltpu.VMEM((16, LANES), F32),
            pltpu.SemaphoreType.DMA,
            pltpu.SemaphoreType.DMA,
            pltpu.SemaphoreType.DMA,
        ],
        compiler_params=pltpu.CompilerParams(collective_id=0, has_side_effects=True),
        name="gather_gains",
    )(coefs.reshape(orders * 2 * directions, width), flags)

    terms = pl.pallas_call(
        functools.partial(work_kernel, width, channels),
        out_shape=jax.ShapeDtypeStruct((devices, directions, LANES), F32),
        in_specs=[smem(), smem()] + [vmem()] * 6,
        out_specs=vmem(),
        scratch_shapes=[
            pltpu.VMEM((local, 2, directions, LANES), F32),
            pltpu.VMEM((flags.shape[0], LANES), F32),
            pltpu.VMEM((4, comps, LANES), F32),
            pltpu.VMEM((LANES, LANES), F32),
            pltpu.VMEM((2, comps, LANES), F32),
            pltpu.VMEM((2, 2, comps, LANES), F32),
            pltpu.VMEM((2, comps, 2 * LANES), jnp.bfloat16),
            pltpu.VMEM((local, 2, directions, 8, LANES), F32),
        ],
        compiler_params=pltpu.CompilerParams(vmem_limit_bytes=48 * 1024 * 1024),
        name="gain_terms",
    )(
        tasks,
        points.reshape(1, local),
        gathered,
        visibility[0],
        station_uvw,
        comp_lm,
        intensity.reshape(1, comps),
        direction.reshape(1, comps),
    )

    out = pl.pallas_call(
        functools.partial(reduce_kernel, sizes),
        out_shape=jax.ShapeDtypeStruct((orders * 2 * directions, width), F32),
        in_specs=[vmem()],
        out_specs=vmem(),
        scratch_shapes=[
            pltpu.VMEM((devices * parts - 1, directions, LANES), F32),
            pltpu.SemaphoreType.DMA,
            pltpu.SemaphoreType.DMA,
        ],
        compiler_params=pltpu.CompilerParams(collective_id=1, has_side_effects=True),
        name="reduce_terms",
    )(terms)
    return out.reshape(orders, 2, directions, width)


def solution(mesh):
    sizes = tuple(mesh.shape[axis] for axis in ("row", "col", "freq"))
    return jax.shard_map(
        functools.partial(on_device, sizes),
        mesh=mesh,
        in_specs=(
            P(("row", "col"), None, "freq", None, None),
            P(("row", "col"), None),
            P(None, ("row", "col")),
            P(),
            P(),
            P(),
            P(),
            P(None, None, None, ("row", "col")),
        ),
        out_specs=P(None, None, None, ("row", "col")),
        check_vma=False,
    )
```

```python
import functools
import math

import jax
import jax.numpy as jnp
import numpy as np
from jax import lax
from jax.experimental import pallas as pl
from jax.experimental.pallas import tpu as pltpu
from jax.sharding import PartitionSpec as P

MESH = pl.DeviceIdType.MESH
LANES = 128
F32 = jnp.float32


def fit_even(function, terms):
    nodes = 0.25 * (1.0 - np.cos(np.pi * (np.arange(400) + 0.5) / 400)) / 2.0
    values = function(np.sqrt(nodes))
    basis = np.stack([nodes**n for n in range(terms)], axis=1)
    return [float(c) for c in np.linalg.lstsq(basis, values, rcond=None)[0]]


SIN_FIT = fit_even(lambda r: np.sin(np.pi * r) / r, 5)
COS_FIT = fit_even(lambda r: np.cos(np.pi * r), 6)


def horner(coefficients, z):
    total = jnp.full_like(z, coefficients[-1])
    for c in coefficients[-2::-1]:
        total = total * z + c
    return total


def turn_cos_sin(turns):
    r = turns - jnp.round(turns)
    z = r * r
    s = horner(SIN_FIT, z) * r
    c = horner(COS_FIT, z)
    return 1.0 - 2.0 * (s * s), 2.0 * (s * c)


def walk(sizes, axes, body):
    count = math.prod(sizes)
    moved = [
        [lax.rem(lax.axis_index(axis) + step, size) for step in range(size)] if count <= 64 else None
        for size, axis in zip(sizes, axes)
    ]

    def far(j, unused):
        rest, where = j + 1, {}
        for size, axis in zip(sizes[::-1], axes[::-1]):
            where[axis] = lax.rem(lax.axis_index(axis) + lax.rem(rest, size), size)
            rest = rest // size
        body(j, where)
        return unused

    if count > 64:
        lax.fori_loop(0, count - 1, far, 0)
        return
    for j in range(count - 1):
        rest, where = j + 1, {}
        for n in range(len(sizes) - 1, -1, -1):
            where[axes[n]] = moved[n][rest % sizes[n]]
            rest = rest // sizes[n]
        body(j, where)


def put_lanes(piece, start):
    rows, width = piece.shape
    parts = []
    if start:
        parts.append(jnp.zeros((rows, start), piece.dtype))
    parts.append(piece)
    if start + width < LANES:
        parts.append(jnp.zeros((rows, LANES - start - width), piece.dtype))
    return jnp.concatenate(parts, axis=1) if len(parts) > 1 else piece


def halves_swapped(x):
    half = x.shape[-1] // 2
    return jnp.concatenate([x[..., half:], x[..., :half]], axis=-1)


def kernel(
    sizes,
    task_ref,
    coef_ref,
    flag_ref,
    vis_hbm,
    uvw_ref,
    lm_ref,
    intensity_ref,
    direction_ref,
    out_ref,
    all_ref,
    part_ref,
    held,
    vis_ref,
    coef_tiles,
    gains,
    flags,
    places,
    sky,
    weight,
    step_table,
    phase,
    x_ref,
    z_ref,
    sums,
    gather_send,
    gather_recv,
    reduce_send,
    reduce_recv,
    vis_sem,
):
    times, local, block = vis_ref.shape[0], vis_ref.shape[1], vis_ref.shape[2]
    comps = sky.shape[1]
    directions = gains.shape[2]
    each = comps // directions
    orders = coef_tiles.shape[0] // 2
    width = coef_ref.shape[1]
    owners = block // width
    channels = local * sizes[2]
    devices = sizes[0] * sizes[1]
    every = ("row", "col", "freq")
    plane = lax.axis_index("row") * sizes[1] + lax.axis_index("col")
    here = {axis: lax.axis_index(axis) for axis in every}

    vis_copy = pltpu.make_async_copy(vis_hbm, vis_ref, vis_sem)
    vis_copy.start()
    barrier = pltpu.get_barrier_semaphore()

    def signal(j, where):
        pl.semaphore_signal(barrier, inc=1, device_id=where, device_id_type=MESH)

    walk(sizes, every, signal)

    for base, ref in ((0, coef_ref), (8, flag_ref)):
        tile = jnp.zeros((8, LANES), F32)
        for g in range(ref.shape[0] // 8):
            tile = tile + put_lanes(ref[8 * g : 8 * g + 8, :].astype(F32), g * width)
        all_ref[plane, base : base + 8, :] = tile

    def entry(n, shape):
        return jnp.broadcast_to(task_ref[0:1, n : n + 1], shape)

    def choose(n, pieces):
        total = jnp.zeros_like(pieces[0])
        for number, piece in enumerate(pieces):
            total = jnp.where(entry(n, piece.shape) == number, piece, total)
        return total


    drow = direction_ref[...].astype(F32)
    count = jnp.zeros((1, comps), F32)
    krow = lax.broadcasted_iota(jnp.int32, (LANES, comps), 1)
    jcol = lax.broadcasted_iota(jnp.int32, (LANES, comps), 0)
    for j in range(comps // LANES):
        piece = jnp.broadcast_to(drow[:, j * LANES : (j + 1) * LANES], (LANES, LANES))
        column = jnp.transpose(piece)
        column = jnp.concatenate([column] * (comps // LANES), axis=1)
        same = jnp.logical_and(column == drow, jcol + j * LANES < krow)
        count = count + jnp.sum(same.astype(F32), axis=0, keepdims=True)
    place = drow * each + count
    east, north = lm_ref[0:1, :], lm_ref[1:2, :]
    depth = jnp.sqrt(1.0 - east * east - north * north) - 1.0
    bright = intensity_ref[...]
    for d in range(directions):
        rows = pl.ds(d * each, each)
        found = (lax.broadcasted_iota(jnp.int32, (each, comps), 0) + d * each).astype(F32) == place
        for n, value in enumerate((east, north, depth, bright)):
            column = jnp.sum(jnp.where(found, value, 0.0), axis=1, keepdims=True)
            if n < 3:
                sky[n, rows, :] = jnp.broadcast_to(column, (each, LANES))
            else:
                wide = jnp.broadcast_to(column, (each, LANES))
                mixed = lax.broadcasted_iota(jnp.int32, (each, LANES), 1) < block
                paired = entry(2, (each, LANES)) == 2
                sky[3, rows, :] = jnp.where(paired, jnp.sqrt(wide), jnp.where(mixed, wide, 1.0))

    pl.semaphore_wait(barrier, math.prod(sizes) - 1)

    def send_gains(j, where):
        pltpu.make_async_remote_copy(
            src_ref=all_ref.at[plane],
            dst_ref=all_ref.at[plane],
            send_sem=gather_send,
            recv_sem=gather_recv,
            device_id=where,
            device_id_type=MESH,
        ).start()

    walk(sizes[:2], every[:2], send_gains)

    start = lax.axis_index("freq") * local
    points = [
        (2.0 * (start + f).astype(F32) - (channels - 1)) / (channels - 1) for f in range(local)
    ]
    factor = 1.0 + 0.15 * points[0]
    spacing = 0.15 * 2.0 / (channels - 1)

    def side_tile(n, task_entry, side):
        pieces = []
        for blk in range(uvw_ref.shape[2] // block):
            tile = uvw_ref[n, :, blk // 2 * LANES : (blk // 2 + 1) * LANES]
            pieces.append(tile if blk % 2 == side else halves_swapped(tile))
        return choose(task_entry, pieces)

    def by_time(a, b):
        kind = entry(2, (times, LANES))
        a = jnp.where(kind == 1, a[times:], a[:times])
        b = jnp.where(kind == 0, b[:times], b[times:])
        return jnp.where(lax.broadcasted_iota(jnp.int32, (times, LANES), 1) < block, a, b)

    for n in range(3):
        places[n] = by_time(side_tile(n, 0, 0), side_tile(n, 1, 1))

    def positions(t):
        return [places[n, pl.ds(t, 1), :] for n in range(3)]

    def turns_of(uvw, rows):
        return sky[0, rows, :] * uvw[0] + sky[1, rows, :] * uvw[1] + sky[2, rows, :] * uvw[2]

    def make_base(uvw, d):
        rows = pl.ds(d * each, each)
        c, s = turn_cos_sin(turns_of(uvw, rows) * factor)
        phase[0, 0, rows, :] = c * sky[3, rows, :]
        phase[0, 1, rows, :] = s * sky[3, rows, :]

    def make_step(uvw, d):
        rows = pl.ds(d * each, each)
        c, s = turn_cos_sin(turns_of(uvw, rows) * spacing)
        step_table[0, rows, :] = 2.0 * c
        step_table[1, rows, :] = s

    def make_x(f):
        for d in range(directions):
            rows = pl.ds(d * each, each)
            if f == 0:
                c, s = phase[0, 0, rows, :], phase[0, 1, rows, :]
            else:
                c1, s1 = phase[f - 1, 0, rows, :], phase[f - 1, 1, rows, :]
                twice = step_table[0, rows, :]
                if f == 1:
                    ec, es = 0.5 * twice, step_table[1, rows, :]
                    c = c1 * ec - s1 * es
                    s = s1 * ec + c1 * es
                else:
                    c = c1 * twice - phase[f - 2, 0, rows, :]
                    s = s1 * twice - phase[f - 2, 1, rows, :]
                phase[f, 0, rows, :] = c
                phase[f, 1, rows, :] = s
            gr, gi = gains[f, 0, d : d + 1, :], gains[f, 1, d : d + 1, :]
            x_ref[f, rows, 0:LANES] = (gr * c + gi * s).astype(jnp.bfloat16)
            x_ref[f, rows, LANES : 2 * LANES] = (gi * c - gr * s).astype(jnp.bfloat16)

    def make_z(f):
        x = x_ref[f]
        z_ref[f % 2] = lax.dot_general(
            x, x, (((0,), (0,)), ((), ())), preferred_element_type=F32
        )

    uvw = positions(0)
    for d in range(directions):
        make_base(uvw, d)
        make_step(uvw, d)
    sums[...] = jnp.zeros_like(sums)

    i = lax.broadcasted_iota(jnp.int32, (block, LANES), 0)
    j = lax.broadcasted_iota(jnp.int32, (block, LANES), 1)
    left = j < block
    j = jnp.where(left, j, j - block)
    upper = (i < j).astype(F32)
    lower = (i > j).astype(F32)
    leftf = left.astype(F32)
    paired = entry(2, (block, LANES)) == 2
    pick_a = jnp.where(paired, upper, 1.0)
    pick_b = jnp.where(paired, lower, 0.0)
    unequal = upper + lower
    mask_a = jnp.where(paired, unequal * leftf, 1.0 - leftf)
    mask_b = jnp.where(paired, unequal * (1.0 - leftf), leftf)

    others = all_ref.at[pl.ds(0, devices - 1)]
    gathered = pltpu.make_async_remote_copy(
        src_ref=others,
        dst_ref=others,
        send_sem=gather_send,
        recv_sem=gather_recv,
        device_id=here,
        device_id_type=MESH,
    )
    gathered.wait_send()
    gathered.wait_recv()

    flag_tiles = []
    sent = [
        [
            choose(side, [all_ref[blk * owners + i] for blk in range(devices // owners)])
            for i in range(owners)
        ]
        for side in range(2)
    ]
    for g in range(2 * orders + flag_ref.shape[0] // 8):
        base, at = (0, g) if g < 2 * orders else (8, g - 2 * orders)
        tile = jnp.zeros((8, LANES), F32)
        for side in range(2):
            for i in range(owners):
                piece = sent[side][i][base : base + 8, at * width : (at + 1) * width]
                tile = tile + put_lanes(piece, side * block + i * width)
        if g < 2 * orders:
            coef_tiles[g] = tile
        else:
            flag_tiles.append(tile)
    all_flags = jnp.concatenate(flag_tiles, axis=0)
    flags[...] = by_time(all_flags, all_flags)
    for f in range(local):
        for c in range(2):
            value = coef_tiles[2 * orders - 2 + c]
            for n in range(orders - 2, -1, -1):
                value = value * points[f] + coef_tiles[2 * n + c]
            gains[f, c] = value

    def make_weight(t, unused):
        good = jnp.broadcast_to(flags[pl.ds(t, 1), :], (LANES, LANES))
        both = good * jnp.transpose(good)
        weight[t, 0:block, :] = both[0:block] * mask_a
        weight[t, block : 2 * block, :] = both[block : 2 * block] * mask_b
        return unused

    lax.fori_loop(0, times, make_weight, 0)
    make_x(0)
    make_z(0)
    make_x(1)
    vis_copy.wait()

    def residual(t, f):
        v = vis_ref[t, f].astype(F32)
        turned = jnp.transpose(jnp.concatenate([v, v], axis=0))
        swapped = halves_swapped(v)
        real, imag = jnp.where(left, v, swapped), jnp.where(left, swapped, v)
        z = z_ref[f % 2]
        model_r = z[0:LANES, 0:LANES] + z[LANES:, LANES:]
        model_i = z[0:LANES, LANES:] - z[LANES:, 0:LANES]
        parts_r, parts_i = [], []
        for side, pick in ((0, pick_a), (1, pick_b)):
            rows = slice(side * block, (side + 1) * block)
            want = pick > 0.5
            vr = jnp.where(want, real, turned[0:block])
            vi = jnp.where(want, -imag, turned[block:])
            w = weight[t, rows, :]
            parts_r.append(w * (vr - model_r[rows]))
            parts_i.append(w * (vi - model_i[rows]))
        er = jnp.concatenate(parts_r, axis=0).astype(jnp.bfloat16)
        ei = jnp.concatenate(parts_i, axis=0).astype(jnp.bfloat16)
        return jnp.concatenate(
            [jnp.concatenate([er, ei], axis=1), jnp.concatenate([-ei, er], axis=1)], axis=0
        )

    def one_time(t, unused):
        later = positions(lax.rem(t + 1, times))
        spread = local >= 8
        for f in range(local):
            e = residual(t, f)
            h = jnp.dot(x_ref[f], e, preferred_element_type=F32)
            make_z((f + 1) % local)
            if f + 2 < local:
                make_x(f + 2)
            for d in range(directions):
                rows = slice(d * each, (d + 1) * each)
                c, s = phase[f, 0, rows, :], phase[f, 1, rows, :]
                hr, hi = h[rows, 0:LANES], h[rows, LANES:]
                tr = jnp.sum((c * hr - s * hi).reshape(each // 8, 8, LANES), axis=0)
                ti = jnp.sum((c * hi + s * hr).reshape(each // 8, 8, LANES), axis=0)
                sums[f, 0, d] += tr
                sums[f, 1, d] += ti
            for d in range(directions):
                if (f == 1 + d * (local - 3) // directions) if spread else f == local - 2:
                    make_base(later, d)
                if f == local - 2:
                    make_step(later, d)
            if f + 2 >= local:
                make_x(f + 2 - local)
        return unused

    lax.fori_loop(0, times, one_time, 0)

    scale = -1.0 / math.sqrt(2 * times * channels * devices * width)
    tiles = [None] * (2 * orders)
    for f in range(local):
        for c in range(2):
            total = jnp.sum(sums[f, c], axis=1) * scale
            for n in range(orders):
                old = tiles[2 * n + c]
                tiles[2 * n + c] = total if old is None else old + total
                total = total * points[f]
    for i in range(owners):
        packed = []
        for side in range(2):
            at = side * block + i * width
            pieces = [tiles[g][:, at : at + width] for g in range(2 * orders)]
            packed.append(put_lanes(jnp.concatenate(pieces, axis=1), 0))
        for blk in range(devices // owners):
            in_first = entry(0, packed[0].shape) == blk
            in_second = entry(1, packed[1].shape) == blk
            part_ref[blk * owners + i] = jnp.where(in_first, packed[0], 0.0) + jnp.where(
                in_second, packed[1], 0.0
            )

    def send_terms(j, where):
        pltpu.make_async_remote_copy(
            src_ref=part_ref.at[where["row"] * sizes[1] + where["col"]],
            dst_ref=held.at[j],
            send_sem=reduce_send,
            recv_sem=reduce_recv,
            device_id=where,
            device_id_type=MESH,
        ).start()

    walk(sizes, every, send_terms)
    arrived = pltpu.make_async_remote_copy(
        src_ref=held,
        dst_ref=held,
        send_sem=reduce_send,
        recv_sem=reduce_recv,
        device_id=here,
        device_id_type=MESH,
    )
    arrived.wait_recv()
    total = part_ref[plane] + jnp.sum(held[...], axis=0)
    for g in range(2 * orders):
        out_ref[8 * g : 8 * g + 8, :] = total[:, g * width : (g + 1) * width]
    arrived.wait_send()


def on_device(sizes, visibility, tasks, flags, station_uvw, comp_lm, intensity, direction, coefs):
    devices = sizes[0] * sizes[1]
    orders, unused, directions, width = coefs.shape
    unused, times, local, block, unused = visibility.shape
    comps = direction.shape[0]
    vmem = pl.BlockSpec(memory_space=pltpu.VMEM)
    out = pl.pallas_call(
        functools.partial(kernel, sizes),
        out_shape=jax.ShapeDtypeStruct((orders * 2 * directions, width), F32),
        in_specs=[
            vmem,
            vmem,
            vmem,
            pl.BlockSpec(memory_space=pl.ANY),
        ]
        + [vmem] * 4,
        out_specs=vmem,
        scratch_shapes=[
            pltpu.VMEM((devices, 16, LANES), F32),
            pltpu.VMEM((devices, directions, LANES), F32),
            pltpu.VMEM((devices * sizes[2] - 1, directions, LANES), F32),
            pltpu.VMEM((times, local, block, 2 * block), jnp.bfloat16),
            pltpu.VMEM((2 * orders, directions, LANES), F32),
            pltpu.VMEM((local, 2, directions, LANES), F32),
            pltpu.VMEM((times, LANES), F32),
            pltpu.VMEM((3, times, LANES), F32),
            pltpu.VMEM((4, comps, LANES), F32),
            pltpu.VMEM((times, LANES, LANES), F32),
            pltpu.VMEM((2, comps, LANES), F32),
            pltpu.VMEM((local, 2, comps, LANES), F32),
            pltpu.VMEM((local, comps, 2 * LANES), jnp.bfloat16),
            pltpu.VMEM((2, 2 * LANES, 2 * LANES), F32),
            pltpu.VMEM((local, 2, directions, 8, LANES), F32),
        ]
        + [pltpu.SemaphoreType.DMA] * 5,
        compiler_params=pltpu.CompilerParams(
            collective_id=0, has_side_effects=True, vmem_limit_bytes=40 * 1024 * 1024
        ),
        name="gain_gradient",
    )(
        tasks,
        coefs.reshape(orders * 2 * directions, width),
        flags,
        visibility[0],
        jnp.transpose(station_uvw, (1, 0, 2)),
        comp_lm,
        intensity.reshape(1, comps),
        direction.reshape(1, comps),
    )
    return out.reshape(orders, 2, directions, width)


def solution(mesh):
    sizes = tuple(mesh.shape[axis] for axis in ("row", "col", "freq"))
    return jax.shard_map(
        functools.partial(on_device, sizes),
        mesh=mesh,
        in_specs=(
            P(("row", "col"), None, "freq", None, None),
            P(("row", "col"), None),
            P(None, ("row", "col")),
            P(),
            P(),
            P(),
            P(),
            P(None, None, None, ("row", "col")),
        ),
        out_specs=P(None, None, None, ("row", "col")),
        check_vma=False,
    )
```

```python
import functools
import math

import jax
import jax.numpy as jnp
import numpy as np
from jax import lax
from jax.experimental import pallas as pl
from jax.experimental.pallas import tpu as pltpu
from jax.sharding import PartitionSpec as P

MESH = pl.DeviceIdType.MESH
LANES = 128
F32 = jnp.float32


def fit_even(function, terms):
    nodes = 0.25 * (1.0 - np.cos(np.pi * (np.arange(400) + 0.5) / 400)) / 2.0
    values = function(np.sqrt(nodes))
    basis = np.stack([nodes**n for n in range(terms)], axis=1)
    return [float(c) for c in np.linalg.lstsq(basis, values, rcond=None)[0]]


SIN_FIT = fit_even(lambda r: np.sin(np.pi * r) / r, 5)
COS_FIT = fit_even(lambda r: np.cos(np.pi * r), 5)


def horner(coefficients, z):
    total = jnp.full_like(z, coefficients[-1])
    for c in coefficients[-2::-1]:
        total = total * z + c
    return total


def turn_cos_sin(turns):
    r = turns - jnp.round(turns)
    z = r * r
    s = horner(SIN_FIT, z) * r
    c = horner(COS_FIT, z)
    return 1.0 - 2.0 * (s * s), 2.0 * (s * c)


def walk(sizes, axes, body):
    count = math.prod(sizes)
    moved = [
        [lax.rem(lax.axis_index(axis) + step, size) for step in range(size)] if count <= 64 else None
        for size, axis in zip(sizes, axes)
    ]

    def far(j, unused):
        rest, where = j + 1, {}
        for size, axis in zip(sizes[::-1], axes[::-1]):
            where[axis] = lax.rem(lax.axis_index(axis) + lax.rem(rest, size), size)
            rest = rest // size
        body(j, where)
        return unused

    if count > 64:
        lax.fori_loop(0, count - 1, far, 0)
        return
    for j in range(count - 1):
        rest, where = j + 1, {}
        for n in range(len(sizes) - 1, -1, -1):
            where[axes[n]] = moved[n][rest % sizes[n]]
            rest = rest // sizes[n]
        body(j, where)


def put_lanes(piece, start):
    rows, width = piece.shape
    parts = []
    if start:
        parts.append(jnp.zeros((rows, start), piece.dtype))
    parts.append(piece)
    if start + width < LANES:
        parts.append(jnp.zeros((rows, LANES - start - width), piece.dtype))
    return jnp.concatenate(parts, axis=1) if len(parts) > 1 else piece


def halves_swapped(x):
    half = x.shape[-1] // 2
    return jnp.concatenate([x[..., half:], x[..., :half]], axis=-1)


def kernel(
    sizes,
    task_hbm,
    coef_hbm,
    flag_hbm,
    direction_hbm,
    lm_hbm,
    intensity_hbm,
    uvw_hbm,
    vis_hbm,
    out_ref,
    task_ref,
    coef_ref,
    flag_ref,
    direction_ref,
    lm_ref,
    intensity_ref,
    uvw_ref,
    vis_ref,
    all_ref,
    part_ref,
    held,
    summed,
    held_sums,
    coef_tiles,
    gains,
    flags,
    places,
    sky,
    weight,
    step_table,
    turned_by,
    phase,
    x_ref,
    z_ref,
    sums,
    gather_send,
    gather_recv,
    reduce_send,
    reduce_recv,
    last_send,
    last_recv,
    load_sems,
):
    times, local, block = vis_ref.shape[0], vis_ref.shape[1], vis_ref.shape[2]
    comps = sky.shape[1]
    directions = gains.shape[2]
    each = comps // directions
    orders = coef_tiles.shape[0] // 2
    width = coef_ref.shape[1]
    owners = block // width
    channels = local * sizes[2]
    devices = sizes[0] * sizes[1]
    every = ("row", "col", "freq")
    plane = lax.axis_index("row") * sizes[1] + lax.axis_index("col")
    here = {axis: lax.axis_index(axis) for axis in every}

    loads = [
        pltpu.make_async_copy(source, target, load_sems.at[n])
        for n, (source, target) in enumerate(
            (
                (coef_hbm, coef_ref),
                (flag_hbm, flag_ref),
                (direction_hbm, direction_ref),
                (task_hbm, task_ref),
                (lm_hbm, lm_ref),
                (intensity_hbm, intensity_ref),
                (uvw_hbm, uvw_ref),
                (vis_hbm, vis_ref),
            )
        )
    ]
    for load in loads:
        load.start()
    barrier = pltpu.get_barrier_semaphore()

    def signal(j, where):
        pl.semaphore_signal(barrier, inc=1, device_id=where, device_id_type=MESH)

    walk(sizes[:2], every[:2], signal)
    walk(sizes[2:], every[2:], signal)

    for load in loads[:-1]:
        load.wait()

    for base, ref in ((0, coef_ref), (8, flag_ref)):
        tile = jnp.zeros((8, LANES), F32)
        for g in range(ref.shape[0] // 8):
            tile = tile + put_lanes(ref[8 * g : 8 * g + 8, :].astype(F32), g * width)
        all_ref[plane, base : base + 8, :] = tile

    def entry(n, shape):
        return jnp.broadcast_to(task_ref[0:1, n : n + 1], shape)

    def choose(n, pieces):
        total = jnp.zeros_like(pieces[0])
        for number, piece in enumerate(pieces):
            total = jnp.where(entry(n, piece.shape) == number, piece, total)
        return total


    start = lax.axis_index("freq") * local
    points = [
        (2.0 * (start + f).astype(F32) - (channels - 1)) / (channels - 1) for f in range(local)
    ]
    factor = 1.0 + 0.15 * points[0]

    drow = direction_ref[...].astype(F32)
    count = jnp.zeros((1, comps), F32)
    krow = lax.broadcasted_iota(jnp.int32, (LANES, comps), 1)
    jcol = lax.broadcasted_iota(jnp.int32, (LANES, comps), 0)
    for j in range(comps // LANES):
        piece = jnp.broadcast_to(drow[:, j * LANES : (j + 1) * LANES], (LANES, LANES))
        column = jnp.transpose(piece)
        column = jnp.concatenate([column] * (comps // LANES), axis=1)
        same = jnp.logical_and(column == drow, jcol + j * LANES < krow)
        count = count + jnp.sum(same.astype(F32), axis=0, keepdims=True)
    place = drow * each + count
    east, north = lm_ref[0:1, :], lm_ref[1:2, :]
    depth = jnp.sqrt(1.0 - east * east - north * north) - 1.0
    bright = intensity_ref[...]
    for d in range(directions):
        rows = pl.ds(d * each, each)
        found = (lax.broadcasted_iota(jnp.int32, (each, comps), 0) + d * each).astype(F32) == place
        for n, value in enumerate((east, north, depth, bright)):
            column = jnp.sum(jnp.where(found, value, 0.0), axis=1, keepdims=True)
            if n < 3:
                sky[n, rows, :] = jnp.broadcast_to(column * factor, (each, LANES))
            else:
                wide = jnp.broadcast_to(column, (each, LANES))
                mixed = lax.broadcasted_iota(jnp.int32, (each, LANES), 1) < block
                paired = entry(2, (each, LANES)) == 2
                sky[3, rows, :] = jnp.where(paired, jnp.sqrt(wide), jnp.where(mixed, wide, 1.0))

    pl.semaphore_wait(barrier, devices - 1 + sizes[2] - 1)

    def send_gains(j, where):
        pltpu.make_async_remote_copy(
            src_ref=all_ref.at[plane],
            dst_ref=all_ref.at[plane],
            send_sem=gather_send,
            recv_sem=gather_recv,
            device_id=where,
            device_id_type=MESH,
        ).start()

    walk(sizes[:2], every[:2], send_gains)

    spacing = 0.15 * 2.0 / (channels - 1) / factor

    def side_tile(n, task_entry, side):
        pieces = []
        for blk in range(uvw_ref.shape[2] // block):
            tile = uvw_ref[n, :, blk // 2 * LANES : (blk // 2 + 1) * LANES]
            pieces.append(tile if blk % 2 == side else halves_swapped(tile))
        return choose(task_entry, pieces)

    def by_time(a, b):
        kind = entry(2, (times, LANES))
        a = jnp.where(kind == 1, a[times:], a[:times])
        b = jnp.where(kind == 0, b[:times], b[times:])
        return jnp.where(lax.broadcasted_iota(jnp.int32, (times, LANES), 1) < block, a, b)

    for n in range(3):
        places[n] = by_time(side_tile(n, 0, 0), side_tile(n, 1, 1))

    def positions(t):
        return [places[n, pl.ds(t, 1), :] for n in range(3)]

    def turns_of(uvw, rows):
        return sky[0, rows, :] * uvw[0] + sky[1, rows, :] * uvw[1] + sky[2, rows, :] * uvw[2]

    def make_base(uvw, d):
        rows = pl.ds(d * each, each)
        turns = turns_of(uvw, rows)
        turned_by[rows, :] = turns
        c, s = turn_cos_sin(turns)
        phase[0, 0, rows, :] = c * sky[3, rows, :]
        phase[0, 1, rows, :] = s * sky[3, rows, :]

    def make_step(d):
        rows = pl.ds(d * each, each)
        c, s = turn_cos_sin(turned_by[rows, :] * spacing)
        step_table[0, rows, :] = 2.0 * c
        step_table[1, rows, :] = s

    def make_x(f):
        for d in range(directions):
            rows = pl.ds(d * each, each)
            if f == 0:
                c, s = phase[0, 0, rows, :], phase[0, 1, rows, :]
            else:
                c1, s1 = phase[f - 1, 0, rows, :], phase[f - 1, 1, rows, :]
                twice = step_table[0, rows, :]
                if f == 1:
                    ec, es = 0.5 * twice, step_table[1, rows, :]
                    c = c1 * ec - s1 * es
                    s = s1 * ec + c1 * es
                else:
                    c = c1 * twice - phase[f - 2, 0, rows, :]
                    s = s1 * twice - phase[f - 2, 1, rows, :]
                phase[f, 0, rows, :] = c
                phase[f, 1, rows, :] = s
            gr, gi = gains[f, 0, d : d + 1, :], gains[f, 1, d : d + 1, :]
            x_ref[f, rows, 0:LANES] = (gr * c + gi * s).astype(jnp.bfloat16)
            x_ref[f, rows, LANES : 2 * LANES] = (gi * c - gr * s).astype(jnp.bfloat16)

    def make_z(f):
        x = x_ref[f]
        z_ref[f % 2] = lax.dot_general(
            x, x, (((0,), (0,)), ((), ())), preferred_element_type=F32
        )

    uvw = positions(0)
    for d in range(directions):
        make_base(uvw, d)
        make_step(d)
    sums[...] = jnp.zeros_like(sums)

    i = lax.broadcasted_iota(jnp.int32, (block, LANES), 0)
    j = lax.broadcasted_iota(jnp.int32, (block, LANES), 1)
    left = j < block
    j = jnp.where(left, j, j - block)
    upper = (i < j).astype(F32)
    lower = (i > j).astype(F32)
    leftf = left.astype(F32)
    paired = entry(2, (block, LANES)) == 2
    pick_a = jnp.where(paired, upper, 1.0)
    pick_b = jnp.where(paired, lower, 0.0)
    unequal = upper + lower
    mask_a = jnp.where(paired, unequal * leftf, 1.0 - leftf)
    mask_b = jnp.where(paired, unequal * (1.0 - leftf), leftf)

    others = all_ref.at[pl.ds(0, devices - 1)]
    gathered = pltpu.make_async_remote_copy(
        src_ref=others,
        dst_ref=others,
        send_sem=gather_send,
        recv_sem=gather_recv,
        device_id=here,
        device_id_type=MESH,
    )
    gathered.wait_send()
    gathered.wait_recv()

    flag_tiles = []
    sent = [
        [
            choose(side, [all_ref[blk * owners + i] for blk in range(devices // owners)])
            for i in range(owners)
        ]
        for side in range(2)
    ]
    for g in range(2 * orders + flag_ref.shape[0] // 8):
        base, at = (0, g) if g < 2 * orders else (8, g - 2 * orders)
        tile = jnp.zeros((8, LANES), F32)
        for side in range(2):
            for i in range(owners):
                piece = sent[side][i][base : base + 8, at * width : (at + 1) * width]
                tile = tile + put_lanes(piece, side * block + i * width)
        if g < 2 * orders:
            coef_tiles[g] = tile
        else:
            flag_tiles.append(tile)
    all_flags = jnp.concatenate(flag_tiles, axis=0)
    flags[...] = by_time(all_flags, all_flags)
    for f in range(local):
        for c in range(2):
            value = coef_tiles[2 * orders - 2 + c]
            for n in range(orders - 2, -1, -1):
                value = value * points[f] + coef_tiles[2 * n + c]
            gains[f, c] = value

    def make_weight(t, unused):
        good = jnp.broadcast_to(flags[pl.ds(t, 1), :], (LANES, LANES))
        both = good * jnp.transpose(good)
        weight[t, 0:block, :] = both[0:block] * mask_a
        weight[t, block : 2 * block, :] = both[block : 2 * block] * mask_b
        return unused

    lax.fori_loop(0, times, make_weight, 0)
    make_x(0)
    make_z(0)
    make_x(1)
    loads[-1].wait()

    def residual(t, f):
        v = vis_ref[t, f].astype(F32)
        turned = jnp.transpose(jnp.concatenate([v, v], axis=0))
        swapped = halves_swapped(v)
        real, imag = jnp.where(left, v, swapped), jnp.where(left, swapped, v)
        z = z_ref[f % 2]
        model_r = z[0:LANES, 0:LANES] + z[LANES:, LANES:]
        model_i = z[0:LANES, LANES:] - z[LANES:, 0:LANES]
        parts_r, parts_i = [], []
        for side, pick in ((0, pick_a), (1, pick_b)):
            rows = slice(side * block, (side + 1) * block)
            want = pick > 0.5
            vr = jnp.where(want, real, turned[0:block])
            vi = jnp.where(want, -imag, turned[block:])
            w = weight[t, rows, :]
            parts_r.append(w * (vr - model_r[rows]))
            parts_i.append(w * (vi - model_i[rows]))
        er = jnp.concatenate(parts_r, axis=0).astype(jnp.bfloat16)
        ei = jnp.concatenate(parts_i, axis=0).astype(jnp.bfloat16)
        return jnp.concatenate(
            [jnp.concatenate([er, ei], axis=1), jnp.concatenate([-ei, er], axis=1)], axis=0
        )

    def one_time(t, unused):
        later = positions(lax.rem(t + 1, times))
        spread = local >= 8
        for f in range(local):
            e = residual(t, f)
            h = jnp.dot(x_ref[f], e, preferred_element_type=F32)
            make_z((f + 1) % local)
            if f + 2 < local:
                make_x(f + 2)
            for d in range(directions):
                rows = slice(d * each, (d + 1) * each)
                c, s = phase[f, 0, rows, :], phase[f, 1, rows, :]
                hr, hi = h[rows, 0:LANES], h[rows, LANES:]
                tr = jnp.sum((c * hr - s * hi).reshape(each // 8, 8, LANES), axis=0)
                ti = jnp.sum((c * hi + s * hr).reshape(each // 8, 8, LANES), axis=0)
                sums[f, 0, d] += tr
                sums[f, 1, d] += ti
            for d in range(directions):
                if (f == 1 + d * (local - 3) // directions) if spread else f == local - 2:
                    make_base(later, d)
                if f == local - 2:
                    make_step(d)
            if f + 2 >= local:
                make_x(f + 2 - local)
        return unused

    lax.fori_loop(0, times, one_time, 0)

    scale = -1.0 / math.sqrt(2 * times * channels * devices * width)
    tiles = [None] * (2 * orders)
    for f in range(local):
        for c in range(2):
            total = jnp.sum(sums[f, c], axis=1) * scale
            for n in range(orders):
                old = tiles[2 * n + c]
                tiles[2 * n + c] = total if old is None else old + total
                total = total * points[f]
    for i in range(owners):
        packed = []
        for side in range(2):
            at = side * block + i * width
            pieces = [tiles[g][:, at : at + width] for g in range(2 * orders)]
            packed.append(put_lanes(jnp.concatenate(pieces, axis=1), 0))
        for blk in range(devices // owners):
            in_first = entry(0, packed[0].shape) == blk
            in_second = entry(1, packed[1].shape) == blk
            part_ref[blk * owners + i] = jnp.where(in_first, packed[0], 0.0) + jnp.where(
                in_second, packed[1], 0.0
            )

    def send_terms(j, where):
        pltpu.make_async_remote_copy(
            src_ref=part_ref.at[where["row"] * sizes[1] + where["col"]],
            dst_ref=held.at[j],
            send_sem=reduce_send,
            recv_sem=reduce_recv,
            device_id=where,
            device_id_type=MESH,
        ).start()

    walk(sizes[:2], every[:2], send_terms)
    arrived = pltpu.make_async_remote_copy(
        src_ref=held,
        dst_ref=held,
        send_sem=reduce_send,
        recv_sem=reduce_recv,
        device_id=here,
        device_id_type=MESH,
    )
    arrived.wait_recv()
    summed[...] = part_ref[plane] + jnp.sum(held[...], axis=0)

    def send_sum(j, where):
        pltpu.make_async_remote_copy(
            src_ref=summed,
            dst_ref=held_sums.at[j],
            send_sem=last_send,
            recv_sem=last_recv,
            device_id=where,
            device_id_type=MESH,
        ).start()

    walk(sizes[2:], every[2:], send_sum)
    last = pltpu.make_async_remote_copy(
        src_ref=held_sums,
        dst_ref=held_sums,
        send_sem=last_send,
        recv_sem=last_recv,
        device_id=here,
        device_id_type=MESH,
    )
    last.wait_recv()
    total = summed[...] + jnp.sum(held_sums[...], axis=0)
    for g in range(2 * orders):
        out_ref[8 * g : 8 * g + 8, :] = total[:, g * width : (g + 1) * width]
    last.wait_send()
    arrived.wait_send()


def on_device(sizes, visibility, tasks, flags, station_uvw, comp_lm, intensity, direction, coefs):
    devices = sizes[0] * sizes[1]
    orders, unused, directions, width = coefs.shape
    unused, times, local, block, unused = visibility.shape
    comps = direction.shape[0]
    inputs = (
        tasks,
        coefs.reshape(orders * 2 * directions, width),
        flags,
        direction.reshape(1, comps),
        comp_lm,
        intensity.reshape(1, comps),
        jnp.transpose(station_uvw, (1, 0, 2)),
        visibility[0],
    )
    out = pl.pallas_call(
        functools.partial(kernel, sizes),
        out_shape=jax.ShapeDtypeStruct((orders * 2 * directions, width), F32),
        in_specs=[pl.BlockSpec(memory_space=pltpu.HBM)] * len(inputs),
        out_specs=pl.BlockSpec(memory_space=pltpu.VMEM),
        scratch_shapes=[pltpu.VMEM(value.shape, value.dtype) for value in inputs]
        + [
            pltpu.VMEM((devices, 16, LANES), F32),
            pltpu.VMEM((devices, directions, LANES), F32),
            pltpu.VMEM((devices - 1, directions, LANES), F32),
            pltpu.VMEM((directions, LANES), F32),
            pltpu.VMEM((sizes[2] - 1, directions, LANES), F32),
            pltpu.VMEM((2 * orders, directions, LANES), F32),
            pltpu.VMEM((local, 2, directions, LANES), F32),
            pltpu.VMEM((times, LANES), F32),
            pltpu.VMEM((3, times, LANES), F32),
            pltpu.VMEM((4, comps, LANES), F32),
            pltpu.VMEM((times, LANES, LANES), F32),
            pltpu.VMEM((2, comps, LANES), F32),
            pltpu.VMEM((comps, LANES), F32),
            pltpu.VMEM((local, 2, comps, LANES), F32),
            pltpu.VMEM((local, comps, 2 * LANES), jnp.bfloat16),
            pltpu.VMEM((2, 2 * LANES, 2 * LANES), F32),
            pltpu.VMEM((local, 2, directions, 8, LANES), F32),
        ]
        + [pltpu.SemaphoreType.DMA] * 6
        + [pltpu.SemaphoreType.DMA((len(inputs),))],
        compiler_params=pltpu.CompilerParams(
            collective_id=0, has_side_effects=True, vmem_limit_bytes=60 * 1024 * 1024
        ),
        name="gain_gradient",
    )(*inputs)
    return out.reshape(orders, 2, directions, width)


def solution(mesh):
    sizes = tuple(mesh.shape[axis] for axis in ("row", "col", "freq"))
    return jax.shard_map(
        functools.partial(on_device, sizes),
        mesh=mesh,
        in_specs=(
            P(("row", "col"), None, "freq", None, None),
            P(("row", "col"), None),
            P(None, ("row", "col")),
            P(),
            P(),
            P(),
            P(),
            P(None, None, None, ("row", "col")),
        ),
        out_specs=P(None, None, None, ("row", "col")),
        check_vma=False,
    )
```
